1024 devices in a mesh: owner: 16 (over y, core), split: 16 (over z), rep: 4 (over x).
Axes of the slice: x: 4, y: 8, z: 16, core: 2. Of those that a mesh axis runs over, the one named last changes fastest.
Arguments:
- embeddings: bfloat16 [196608, 1024], P(('rep', 'owner', 'split')), parts along dimension 0, may hold values from -20 to 20
- cluster: int32 [196608], P(('rep', 'owner', 'split')), parts along dimension 0, may hold values from 0 to 15, as said below
- rank: int32 [196608], P(('rep', 'owner', 'split')), parts along dimension 0, may hold values from 0 to 49151, each once
Outputs:
- best: float32 [196608], P(('rep', 'owner', 'split')), parts along dimension 0
The draws below stay inside these ranges and needn't reach their ends.
There are 4 independent parts, one for each index of `rep`. The reference program is written for one: setup_inputs(seed, part) draws one part's arguments, and reference() takes and returns one part's arrays. A program takes and returns all parts, laid end to end along the dimension named above; each array names one. Nothing has to cross between parts.
Inputs may be any that keep to these rules, and one draw needn't show every extreme that they name: `cluster`: cluster c belongs to owner index c mod 16. Among the 192 rows of one device at most 18 belong to clusters of one owner index, and exactly 18 for some owner index on every device.
All inputs are finite; a program needn't handle non-finite values.
Results may differ from the reference program's by a relative error of at most 0.00048.
Values may be sent and summed in bfloat16 or wider, within the bound.
No kernel may reach another device: no remote copies, remote signals or barrier semaphores. Data moves between devices by JAX's collectives and lax.ppermute only.
A program may use at most 32 MiB of HBM per device.

```python
import math
import jax
import jax.numpy as jnp
from jax import lax

D = 1024
ROWS_DEV = 192
CLUST_OWN = 1
CAP = 18
ROWS = 49152
CLUSTERS = 16


def shared_clusters(key):
    owners = CLUSTERS // CLUST_OWN
    blocks = ROWS // ROWS_DEV
    columns = blocks // owners
    total_slots = owners * CAP
    second = jax.random.fold_in(jax.random.fold_in(key, 101), 1)
    third = jax.random.fold_in(jax.random.fold_in(key, 101), 2)
    fourth = jax.random.fold_in(jax.random.fold_in(key, 101), 3)
    fifth = jax.random.fold_in(jax.random.fold_in(key, 101), 4)
    full_owner = jax.random.randint(second, (columns,), 0, owners)
    block_full = jnp.tile(full_owner, owners)
    scores = jax.vmap(lambda k: jax.random.permutation(k, total_slots))(jax.random.split(third, blocks))
    slot_owner = jnp.arange(total_slots) // CAP
    scores = jnp.where(slot_owner[None, :] == block_full[:, None], -1, scores)
    chosen = jnp.argsort(scores, axis=1, stable=True)[:, :ROWS_DEV]
    shuffle = jax.vmap(lambda k: jax.random.permutation(k, ROWS_DEV))(jax.random.split(fourth, blocks))
    chosen = jnp.take_along_axis(chosen, shuffle, axis=1)
    target = chosen // CAP
    which = jax.random.randint(fifth, (blocks, ROWS_DEV), 0, CLUST_OWN)
    member = target + owners * which
    return member.reshape(ROWS).astype(jnp.int32)


def draw_cluster(key, part):
    return shared_clusters(key)


def draw_embeddings(key, part):
    member = shared_clusters(key)
    key = jax.random.fold_in(key, 7)
    keys = jax.random.split(key, 5)
    variants = max(1, ROWS // (CLUSTERS * 4))
    centre = jax.random.normal(keys[0], (CLUSTERS, D), jnp.float32)
    table = jax.random.normal(keys[1], (CLUSTERS * variants, D), jnp.float32)
    variant = member * variants + jax.random.randint(keys[2], (ROWS,), 0, variants)
    weight = jax.random.uniform(keys[3], (ROWS, 1), jnp.float32, 0.5, 2.5)
    noise = jax.random.normal(keys[4], (ROWS, D), jnp.float32)
    values = 0.5 * centre[member] + weight * table[variant] + noise
    return jnp.clip(values, -20.0, 20.0).astype(jnp.bfloat16)


def setup_inputs(seed: int = 0, part: int = 0) -> dict:
    arg_keys = jax.random.split(jax.random.key(seed), 4)
    part_keys = jax.random.split(jax.random.fold_in(arg_keys[3], part), 4)
    return {
        "embeddings": draw_embeddings(jax.random.fold_in(jax.random.fold_in(arg_keys[3], part), 71), part),
        "cluster": draw_cluster(jax.random.fold_in(jax.random.fold_in(arg_keys[3], part), 71), part),
        "rank": jax.random.permutation(part_keys[2], ROWS).astype(jnp.int32),
    }


def reference(embeddings, cluster, rank):
    wide = embeddings.astype(jnp.float32)
    unit = (wide / jnp.sqrt(lax.optimization_barrier(jnp.sum(wide * wide, axis=1, keepdims=True)) + 1e-06)).astype(jnp.bfloat16)
    unit_wide = unit.astype(jnp.float32)
    block = math.gcd(ROWS, 512)
    count = ROWS // block

    def one_block(index):
        start = (index * block).astype(jnp.int32)
        query = lax.dynamic_slice_in_dim(unit_wide, start, block, 0)
        query_cluster = lax.dynamic_slice_in_dim(cluster, start, block, 0)
        query_rank = lax.dynamic_slice_in_dim(rank, start, block, 0)
        scores = lax.dot_general(query, unit_wide, (((1,), (1,)), ((), ())), precision=lax.Precision.HIGHEST, preferred_element_type=jnp.float32)
        valid = (query_cluster[:, None] == cluster[None, :]) & (rank[None, :] < query_rank[:, None])
        return lax.optimization_barrier(jnp.max(jnp.where(valid, scores, jnp.float32(-1.0)), axis=1))
    result = lax.map(one_block, jnp.arange(count, dtype=jnp.int32))
    return result.reshape(ROWS)
```

```python
import functools

import jax
import jax.numpy as jnp
from jax import lax
from jax.experimental import pallas as pl
from jax.experimental.pallas import tpu as pltpu
from jax.sharding import PartitionSpec as P

MAIN = 16
REM = 2
RANK_TILE = 8
LANES = 128
ABSENT = 256.0

NT = (((1,), (1,)), ((), ()))
NN = (((1,), (0,)), ((), ()))


def dot(left, right, dims):
    return lax.dot_general(left, right, dims, preferred_element_type=jnp.float32)


def iota(shape, dim):
    return lax.broadcasted_iota(jnp.int32, shape, dim)


def to_column(row):
    n = row.shape[1]
    return jnp.sum(jnp.where(iota((n, n), 0) == iota((n, n), 1), row, 0.0), axis=1, keepdims=True)


def to_row(column):
    n = column.shape[0]
    return jnp.sum(jnp.where(iota((n, n), 0) == iota((n, n), 1), column, 0.0), axis=0, keepdims=True)


def pack_kernel(groups, home_ref, emb_ref, cluster_ref, rank_ref, out_ref, place_ref):
    rows, width = emb_ref.shape
    pieces = width // LANES
    home = home_ref[0]
    wide = emb_ref[...].astype(jnp.float32)
    norm = jnp.sqrt(jnp.sum(wide * wide, axis=1, keepdims=True) + 1e-06)
    unit = (wide / norm).astype(jnp.bfloat16)

    target = lax.rem(cluster_ref[...], groups)
    target_column = to_column(target.astype(jnp.float32)).astype(jnp.int32)
    earlier = (target_column == target) & (iota((rows, rows), 0) < iota((rows, rows), 1))
    position = jnp.sum(earlier.astype(jnp.float32), axis=0, keepdims=True).astype(jnp.int32)
    is_main = position < MAIN
    place_ref[...] = jnp.where(
        is_main, home * MAIN + position, groups * MAIN + home * REM + position - MAIN
    )

    slot = jnp.where(is_main, target * MAIN + position, -1)
    placing = (iota((groups * MAIN, rows), 0) == slot).astype(jnp.bfloat16)
    main = dot(placing, unit, NN).astype(jnp.bfloat16)
    for k in range(pieces):
        piece = main[:, k * LANES : (k + 1) * LANES]
        out_ref[:, k * MAIN : (k + 1) * MAIN, :] = piece.reshape(groups, MAIN, LANES)

    spread = pieces * REM
    rest = jnp.zeros((groups * spread, LANES), jnp.float32)
    for k in range(pieces):
        slot = jnp.where(is_main, -1, target * spread + k * REM + position - MAIN)
        placing = (iota((groups * spread, rows), 0) == slot).astype(jnp.bfloat16)
        rest += dot(placing, unit[:, k * LANES : (k + 1) * LANES], NN)

    rank = rank_ref[...]
    high = (rank >> 8).astype(jnp.float32) - ABSENT
    low = (rank & 255).astype(jnp.float32)
    line = iota((groups * RANK_TILE, rows), 0)
    mine = line // RANK_TILE == target
    line = line % RANK_TILE
    band = home * MAIN // LANES
    lane = iota((LANES, rows), 0)
    at_main = (lane == jnp.where(is_main, lax.rem(home * MAIN, LANES) + position, -1)).astype(
        jnp.bfloat16
    )
    at_rest = (lane == jnp.where(is_main, -1, home * REM + position - MAIN)).astype(jnp.bfloat16)

    def values(first):
        value = jnp.where(line == first, high, jnp.where(line == first + 1, low, 0.0))
        return jnp.where(mine, value, 0.0).astype(jnp.bfloat16)

    tile = dot(values(2 * band), at_main, NT) + dot(values(4), at_rest, NT)
    shape = (groups * RANK_TILE, LANES)
    line, lane = iota(shape, 0) % RANK_TILE, iota(shape, 1)
    from_main = (line == 2 * band) & (lane // MAIN == lax.rem(home, LANES // MAIN))
    from_rest = (line == 4) & (lane // REM == home)
    tile += jnp.where(from_main | from_rest, ABSENT, 0.0)
    tail = jnp.concatenate(
        [rest.reshape(groups, spread, LANES), tile.reshape(groups, RANK_TILE, LANES)], axis=1
    )
    out_ref[:, pieces * MAIN :, :] = tail.astype(jnp.bfloat16)


def score_kernel(groups, pieces, targets_ref, *refs):
    counts = (2, 2, 2, 1, 2, 2)
    blocks, at = [], 0
    for count in counts:
        blocks.append(refs[at : at + count])
        at += count
    out_ref, main_ref, rest_ref, query_ref = refs[at:]
    mains, rests, spread = groups * MAIN, groups * REM, pieces * REM
    block_rows = mains + rests

    def unpack(parts, to_main, to_rest, main_at, rest_at):
        tiles, tails, row = 0.0, [], 0
        for part in parts:
            senders = part.shape[0]
            for k in range(pieces):
                to_main[pl.ds(main_at + row, senders * MAIN), k * LANES : (k + 1) * LANES] = part[
                    :, k * MAIN : (k + 1) * MAIN, :
                ].reshape(senders * MAIN, LANES)
            row += senders * MAIN
            tail = part[:, pieces * MAIN :, :].astype(jnp.float32)
            tiles = tiles + jnp.sum(tail[:, spread:, :], axis=0)
            tails.append(tail[:, :spread, :].reshape(senders * spread, LANES).astype(jnp.bfloat16))
        tail = jnp.concatenate(tails, axis=0) if len(tails) > 1 else tails[0]
        shape = (rests, groups * spread)
        line, column = iota(shape, 0), iota(shape, 1)
        for k in range(pieces):
            pick = (column == line // REM * spread + k * REM + line % REM).astype(jnp.bfloat16)
            to_rest[pl.ds(rest_at, rests), k * LANES : (k + 1) * LANES] = dot(pick, tail, NN).astype(
                jnp.bfloat16
            )
        main = [tiles[2 * g : 2 * g + 1] * 256.0 + tiles[2 * g + 1 : 2 * g + 2] for g in range(mains // LANES)]
        return jnp.concatenate(main, axis=1), (tiles[4:5] * 256.0 + tiles[5:6])[:, :rests]

    other, own = blocks[0], blocks[1:]
    main_ranks, rest_ranks = [], []
    for i, parts in enumerate(own):
        main, rest = unpack(parts, main_ref, rest_ref, i * mains, i * rests)
        main_ranks.append(main)
        rest_ranks.append(rest)
    other_main, other_rest = unpack(other, query_ref, query_ref, block_rows, block_rows + mains)
    query_ref[pl.ds(0, mains), :] = main_ref[pl.ds(0, mains), :]
    query_ref[pl.ds(mains, rests), :] = rest_ref[pl.ds(0, rests), :]
    query_ranks = [
        jnp.concatenate([to_column(main_ranks[0]), to_column(rest_ranks[0])], axis=0),
        jnp.concatenate([to_column(other_main), to_column(other_rest)], axis=0),
    ]
    rest_rank = jnp.concatenate(rest_ranks, axis=1)
    window = len(own)

    best_query = [None, None]
    best_main = [None] * window
    best_rest = None
    for q in range(2):
        query = query_ref[pl.ds(q * block_rows, block_rows), :]
        for i in range(window + 1):
            if i < window:
                key, key_rank = main_ref[pl.ds(i * mains, mains), :], main_ranks[i]
            else:
                key, key_rank = rest_ref[...], rest_rank
            scores = dot(query, key, NT)
            lower = key_rank < query_ranks[q]
            found = jnp.max(jnp.where(lower, scores, -1.0), axis=1, keepdims=True)
            best_query[q] = found if best_query[q] is None else jnp.maximum(best_query[q], found)
            if q == 0 and i == 0:
                continue
            back = jnp.where(lower, -1.0, scores)
            if q == 0 and i == window:
                back = jnp.where(iota(back.shape, 1) < rests, -1.0, back)
            found = jnp.max(back, axis=0, keepdims=True)
            if i < window:
                best_main[i] = found if best_main[i] is None else jnp.maximum(best_main[i], found)
            else:
                best_rest = found if best_rest is None else jnp.maximum(best_rest, found)

    queries = [jnp.concatenate([to_row(b[:mains]), to_row(b[mains:])], axis=1) for b in best_query]
    lines = [jnp.concatenate([best_main[i], best_rest[:, i * rests : (i + 1) * rests]], axis=1) for i in range(window)]
    lines[0] = jnp.maximum(lines[0], queries[0])
    lines.append(queries[1])
    targets = out_ref.shape[0]
    line = iota((targets, block_rows), 0)
    out = jnp.full((targets, block_rows), -1.0, jnp.float32)
    for i, value in enumerate(lines):
        out = jnp.where(line == targets_ref[i], value, out)
    pad = out_ref.shape[2] - block_rows
    out = jnp.concatenate([out, jnp.full((targets, pad), -1.0, jnp.float32)], axis=1)
    out_ref[...] = out.reshape(out_ref.shape)


def pick_kernel(groups, arrived_ref, cluster_ref, place_ref, out_ref):
    arrived = arrived_ref[...].reshape(groups, arrived_ref.shape[2])
    rows = place_ref.shape[1]
    place = (iota((arrived.shape[1], rows), 0) == place_ref[...]).astype(jnp.bfloat16)
    found = jnp.zeros((groups, rows), jnp.float32)
    left = arrived
    for _ in range(3):
        term = left.astype(jnp.bfloat16)
        found += dot(term, place, NN)
        left = left - term.astype(jnp.float32)
    target = lax.rem(cluster_ref[...], groups)
    mine = iota((groups, rows), 0) == target
    out_ref[...] = jnp.sum(jnp.where(mine, found, 0.0), axis=0, keepdims=True)


def shards(embeddings, cluster, rank):
    rows, width = embeddings.shape
    owners, groups = lax.axis_size("owner"), lax.axis_size("split")
    pieces = width // LANES
    depth = pieces * (MAIN + REM) + RANK_TILE
    block_rows = groups * (MAIN + REM)
    padded = -(-block_rows // LANES) * LANES
    owner = lax.axis_index("owner").astype(jnp.int32)
    home = lax.axis_index("split").astype(jnp.int32)
    cluster, rank = cluster.reshape(1, rows), rank.reshape(1, rows)
    smem = pl.BlockSpec(memory_space=pltpu.SMEM)
    vmem = pl.BlockSpec(memory_space=pltpu.VMEM)
    params = pltpu.CompilerParams(vmem_limit_bytes=40 * 1024 * 1024)

    packed, place = pl.pallas_call(
        functools.partial(pack_kernel, groups),
        out_shape=(
            jax.ShapeDtypeStruct((groups, depth, LANES), jnp.bfloat16),
            jax.ShapeDtypeStruct((1, rows), jnp.int32),
        ),
        in_specs=[smem, vmem, vmem, vmem],
        out_specs=(vmem, vmem),
        compiler_params=params,
        name="pack",
    )(home.reshape(1), embeddings, cluster, rank)

    block = lax.all_to_all(packed, "split", split_axis=0, concat_axis=0, tiled=True)

    def shift(value, chips):
        return lax.ppermute(value, "owner", [(o, (o + 2 * chips) % owners) for o in range(owners)])

    def swap(value):
        return lax.ppermute(value, "owner", [(o, o ^ 1) for o in range(owners)])

    halves = (block[: groups // 2], block[groups // 2 :])
    back1 = [shift(h, 1) for h in halves]
    ahead1 = [shift(h, -1) for h in halves]
    back2 = [shift(h, 1) for h in back1]
    ahead2 = [shift(h, -1) for h in ahead1]
    other2 = [swap(h) for h in back2]

    chip, core = owner // 2, owner % 2
    chips = owners // 2
    targets = [lax.rem(chip + chips + d, chips) * 2 + core for d in (-2, -1, 0, 1, 2)]
    targets.append(lax.rem(chip + chips - 2, chips) * 2 + 1 - core)
    window = 5
    best = pl.pallas_call(
        functools.partial(score_kernel, groups, pieces),
        out_shape=jax.ShapeDtypeStruct((owners, 1, padded), jnp.float32),
        in_specs=[smem] + [vmem] * 11,
        out_specs=vmem,
        scratch_shapes=[
            pltpu.VMEM((window * groups * MAIN, width), jnp.bfloat16),
            pltpu.VMEM((window * groups * REM, width), jnp.bfloat16),
            pltpu.VMEM((2 * block_rows, width), jnp.bfloat16),
        ],
        compiler_params=params,
        name="score",
    )(jnp.stack(targets), *other2, *back2, *back1, block, *ahead1, *ahead2)

    best = lax.all_to_all(best, "owner", split_axis=0, concat_axis=0, tiled=True)
    best = jnp.broadcast_to(jnp.max(best, axis=0, keepdims=True), (groups, 1, padded))
    arrived = lax.all_to_all(best, "split", split_axis=0, concat_axis=0, tiled=True)

    result = pl.pallas_call(
        functools.partial(pick_kernel, groups),
        out_shape=jax.ShapeDtypeStruct((1, rows), jnp.float32),
        in_specs=[vmem, vmem, vmem],
        out_specs=vmem,
        compiler_params=params,
        name="pick",
    )(arrived, cluster, place)
    return result.reshape(rows)


def solution(mesh):
    return jax.shard_map(
        shards,
        mesh=mesh,
        in_specs=(
            P(("rep", "owner", "split"), None),
            P(("rep", "owner", "split")),
            P(("rep", "owner", "split")),
        ),
        out_specs=P(("rep", "owner", "split")),
        check_vma=False,
    )
```

```python
import functools

import jax
import jax.numpy as jnp
from jax import lax
from jax.experimental import pallas as pl
from jax.experimental.pallas import tpu as pltpu
from jax.sharding import PartitionSpec as P

MAIN = 16
REM = 2
RANK_TILE = 8
LANES = 128
ABSENT = 256.0

NT = (((1,), (1,)), ((), ()))
NN = (((1,), (0,)), ((), ()))


def dot(left, right, dims):
    return lax.dot_general(left, right, dims, preferred_element_type=jnp.float32)


def iota(shape, dim):
    return lax.broadcasted_iota(jnp.int32, shape, dim)


def to_column(row):
    parts = []
    for at in range(0, row.shape[1], LANES):
        part = row[:, at : at + LANES]
        n = part.shape[1]
        same = iota((n, n), 0) == iota((n, n), 1)
        parts.append(jnp.sum(jnp.where(same, part, 0.0), axis=1, keepdims=True))
    return jnp.concatenate(parts, axis=0)


def to_row(column):
    parts = []
    for at in range(0, column.shape[0], LANES):
        part = column[at : at + LANES]
        n = part.shape[0]
        same = iota((n, n), 0) == iota((n, n), 1)
        parts.append(jnp.sum(jnp.where(same, part, 0.0), axis=0, keepdims=True))
    return jnp.concatenate(parts, axis=1)


def pack_kernel(groups, home_ref, emb_ref, cluster_ref, rank_ref, out_ref, place_ref):
    rows, width = emb_ref.shape
    pieces = width // LANES
    home = home_ref[0]
    wide = emb_ref[...].astype(jnp.float32)
    norm = jnp.sqrt(jnp.sum(wide * wide, axis=1, keepdims=True) + 1e-06)
    unit = (wide / norm).astype(jnp.bfloat16)

    target = lax.rem(cluster_ref[...], groups)
    target_column = to_column(target.astype(jnp.float32)).astype(jnp.int32)
    earlier = (target_column == target) & (iota((rows, rows), 0) < iota((rows, rows), 1))
    position = jnp.sum(earlier.astype(jnp.float32), axis=0, keepdims=True).astype(jnp.int32)
    is_main = position < MAIN
    place_ref[...] = jnp.where(
        is_main, home * MAIN + position, groups * MAIN + home * REM + position - MAIN
    )

    slot = jnp.where(is_main, target * MAIN + position, -1)
    placing = (iota((groups * MAIN, rows), 0) == slot).astype(jnp.bfloat16)
    main = dot(placing, unit, NN).astype(jnp.bfloat16)
    for k in range(pieces):
        piece = main[:, k * LANES : (k + 1) * LANES]
        out_ref[:, k * MAIN : (k + 1) * MAIN, :] = piece.reshape(groups, MAIN, LANES)

    spread = pieces * REM
    rest = jnp.zeros((groups * spread, LANES), jnp.float32)
    for k in range(pieces):
        slot = jnp.where(is_main, -1, target * spread + k * REM + position - MAIN)
        placing = (iota((groups * spread, rows), 0) == slot).astype(jnp.bfloat16)
        rest += dot(placing, unit[:, k * LANES : (k + 1) * LANES], NN)

    rank = rank_ref[...]
    high = (rank >> 8).astype(jnp.float32) - ABSENT
    low = (rank & 255).astype(jnp.float32)
    line = iota((groups * RANK_TILE, rows), 0)
    mine = line // RANK_TILE == target
    line = line % RANK_TILE
    band = home * MAIN // LANES
    lane = iota((LANES, rows), 0)
    at_main = (lane == jnp.where(is_main, lax.rem(home * MAIN, LANES) + position, -1)).astype(
        jnp.bfloat16
    )
    at_rest = (lane == jnp.where(is_main, -1, home * REM + position - MAIN)).astype(jnp.bfloat16)

    def values(first):
        value = jnp.where(line == first, high, jnp.where(line == first + 1, low, 0.0))
        return jnp.where(mine, value, 0.0).astype(jnp.bfloat16)

    tile = dot(values(2 * band), at_main, NT) + dot(values(4), at_rest, NT)
    shape = (groups * RANK_TILE, LANES)
    line, lane = iota(shape, 0) % RANK_TILE, iota(shape, 1)
    from_main = (line == 2 * band) & (lane // MAIN == lax.rem(home, LANES // MAIN))
    from_rest = (line == 4) & (lane // REM == home)
    tile += jnp.where(from_main | from_rest, ABSENT, 0.0)
    tail = jnp.concatenate(
        [rest.reshape(groups, spread, LANES), tile.reshape(groups, RANK_TILE, LANES)], axis=1
    )
    out_ref[:, pieces * MAIN :, :] = tail.astype(jnp.bfloat16)


def unpack(parts, scratch, slot):
    main_ref, rest_ref, main_rank_ref, rest_rank_ref = scratch
    width = main_ref.shape[2]
    pieces = width // LANES
    mains, rests, spread = main_ref.shape[1], rest_ref.shape[1], pieces * REM
    row, rest, tile = 0, [], 0.0
    for part in parts:
        senders = part.shape[0]
        for k in range(pieces):
            piece = part[:, k * MAIN : (k + 1) * MAIN, :].reshape(senders * MAIN, LANES)
            main_ref[slot, row : row + senders * MAIN, k * LANES : (k + 1) * LANES] = piece
        row += senders * MAIN
        tail = part[:, pieces * MAIN :, :].astype(jnp.float32)
        rest.append(tail[:, :spread, :].reshape(senders * spread, LANES).astype(jnp.bfloat16))
        tile = tile + jnp.sum(tail[:, spread:, :], axis=0)
    rest = jnp.concatenate(rest, axis=0) if len(rest) > 1 else rest[0]
    line, column = iota((pieces * rests, rest.shape[0]), 0), iota((pieces * rests, rest.shape[0]), 1)
    k, line = line // rests, line % rests
    pick = (column == line // REM * spread + k * REM + line % REM).astype(jnp.bfloat16)
    rest = dot(pick, rest, NN).astype(jnp.bfloat16)
    for k in range(pieces):
        rest_ref[slot, :, k * LANES : (k + 1) * LANES] = rest[k * rests : (k + 1) * rests]
    for g in range(mains // LANES):
        high, low = tile[2 * g : 2 * g + 1], tile[2 * g + 1 : 2 * g + 2]
        main_rank_ref[slot, :, g * LANES : (g + 1) * LANES] = high * 256.0 + low
    rest_rank_ref[slot] = (tile[4:5] * 256.0 + tile[5:6])[:, :rests]


def score(query, key, query_rank, key_rank):
    scores = dot(query, key, NT)
    lower = key_rank < query_rank
    return (
        jnp.max(jnp.where(lower, scores, -1.0), axis=1, keepdims=True),
        jnp.max(jnp.where(key_rank > query_rank, scores, -1.0), axis=0, keepdims=True),
    )


def meet(scratch, slots):
    main_ref, rest_ref, main_rank_ref, rest_rank_ref = scratch
    mains, rests, width = main_ref.shape[1], rest_ref.shape[1], main_ref.shape[2]
    others = slots - 1
    other = main_ref[1:slots].reshape(others * mains, width)
    other_rank = jnp.concatenate([to_column(main_rank_ref[i]) for i in range(1, slots)], axis=0)
    rest = rest_ref[0:slots].reshape(slots * rests, width)
    rest_row = jnp.concatenate([rest_rank_ref[i] for i in range(slots)], axis=1)
    rest_rank = to_column(rest_row)
    pivot, pivot_rank = main_ref[0], main_rank_ref[0]
    best_other, best_pivot = score(other, pivot, other_rank, pivot_rank)
    best_rest, found = score(rest, pivot, rest_rank, pivot_rank)
    best_pivot = jnp.maximum(best_pivot, found)
    found, back = score(other, rest_ref[0], other_rank, rest_row[:, :rests])
    best_other = jnp.maximum(best_other, found)
    best_rest = jnp.maximum(best_rest, score(rest, rest, rest_rank, rest_row)[0])
    best_rest = to_row(best_rest)
    results = [(best_pivot, jnp.maximum(best_rest[:, :rests], back))]
    for i in range(others):
        main = to_row(best_other[i * mains : (i + 1) * mains])
        results.append((main, best_rest[:, (i + 1) * rests : (i + 2) * rests]))
    return results


def keep(out_ref, results):
    for i, (main, rest) in enumerate(results):
        n = main.shape[1] + rest.shape[1]
        out_ref[i : i + 1, :n] = jnp.concatenate([main, rest], axis=1)


def near_kernel(own_ref, other_ref, ahead0_ref, ahead1_ref, out_ref, *scratch):
    main_ref, rest_ref, main_rank_ref, rest_rank_ref = scratch
    unpack([ahead0_ref, ahead1_ref], scratch, 0)
    unpack([own_ref], scratch, 1)
    unpack([other_ref], scratch, 2)
    results = meet(scratch, 3)
    rests, width = rest_ref.shape[1], main_ref.shape[2]
    own, own_rank = main_ref[1], to_column(main_rank_ref[1])
    (main_own, rest_own), (main_other, rest_other) = results[1:]
    own_best, _ = score(own, own, own_rank, main_rank_ref[1])
    found, _ = score(own, main_ref[2], own_rank, main_rank_ref[2])
    own_best = to_row(jnp.maximum(own_best, found))
    rest = rest_ref[1:3].reshape(2 * rests, width)
    rest_rank = to_column(jnp.concatenate([rest_rank_ref[1], rest_rank_ref[2]], axis=1))
    found, back = score(rest, own, rest_rank, main_rank_ref[1])
    found = to_row(found)
    main_own = jnp.maximum(jnp.maximum(main_own, own_best), back)
    rest_own = jnp.maximum(rest_own, found[:, :rests])
    found, back = score(rest_ref[1], main_ref[2], rest_rank[:rests], main_rank_ref[2])
    rest_own = jnp.maximum(rest_own, to_row(found))
    keep(out_ref, [results[0], (main_own, rest_own), (main_other, rest_other)])


def mid_kernel(own_ref, other_ref, ahead0_ref, ahead1_ref, back0_ref, back1_ref, out_ref, *scratch):
    unpack([back0_ref, back1_ref], scratch, 0)
    unpack([own_ref], scratch, 1)
    unpack([other_ref], scratch, 2)
    unpack([ahead0_ref, ahead1_ref], scratch, 3)
    keep(out_ref, meet(scratch, 4))


def late_kernel(
    place_ref, near_ref, mid_ref, back0_ref, back1_ref, far_back0_ref, far_back1_ref, far_ahead0_ref, far_ahead1_ref,
    out_ref, *scratch,
):
    unpack([back0_ref, back1_ref], scratch, 1)
    unpack([far_back0_ref, far_back1_ref], scratch, 2)
    unpack([far_ahead0_ref, far_ahead1_ref], scratch, 0)
    results = meet(scratch, 3)
    mains = results[0][0].shape[1]
    n = mains + results[0][1].shape[1]
    out_ref[...] = jnp.full(out_ref.shape, -1.0, jnp.float32)

    def add(i, values, start, end):
        at = (place_ref[i], slice(None), slice(start, end))
        out_ref[at] = jnp.maximum(out_ref[at], values)

    for i in range(3):
        add(i, near_ref[i : i + 1, :n], 0, n)
    for i in range(4):
        add(3 + i, mid_ref[i : i + 1, :n], 0, n)
    for i, (main, rest) in enumerate(results):
        add(7 + i, main, 0, mains)
        add(7 + i, rest, mains, n)


def pick_kernel(groups, arrived_ref, cluster_ref, place_ref, out_ref):
    arrived = arrived_ref[...].reshape(groups, arrived_ref.shape[2])
    rows = place_ref.shape[1]
    place = (iota((arrived.shape[1], rows), 0) == place_ref[...]).astype(jnp.bfloat16)
    found = jnp.zeros((groups, rows), jnp.float32)
    left = arrived
    for _ in range(3):
        term = left.astype(jnp.bfloat16)
        found += dot(term, place, NN)
        left = left - term.astype(jnp.float32)
    target = lax.rem(cluster_ref[...], groups)
    mine = iota((groups, rows), 0) == target
    out_ref[...] = jnp.sum(jnp.where(mine, found, 0.0), axis=0, keepdims=True)


def shards(embeddings, cluster, rank):
    rows, width = embeddings.shape
    owners, groups = lax.axis_size("owner"), lax.axis_size("split")
    pieces = width // LANES
    depth = pieces * (MAIN + REM) + RANK_TILE
    block_rows = groups * (MAIN + REM)
    padded = -(-block_rows // LANES) * LANES
    owner = lax.axis_index("owner").astype(jnp.int32)
    home = lax.axis_index("split").astype(jnp.int32)
    cluster, rank = cluster.reshape(1, rows), rank.reshape(1, rows)
    smem = pl.BlockSpec(memory_space=pltpu.SMEM)
    vmem = pl.BlockSpec(memory_space=pltpu.VMEM)
    params = pltpu.CompilerParams(vmem_limit_bytes=40 * 1024 * 1024)

    packed, slots = pl.pallas_call(
        functools.partial(pack_kernel, groups),
        out_shape=(
            jax.ShapeDtypeStruct((groups, depth, LANES), jnp.bfloat16),
            jax.ShapeDtypeStruct((1, rows), jnp.int32),
        ),
        in_specs=[smem, vmem, vmem, vmem],
        out_specs=(vmem, vmem),
        compiler_params=params,
        name="pack",
    )(home.reshape(1), embeddings, cluster, rank)

    block = lax.all_to_all(packed, "split", split_axis=0, concat_axis=0, tiled=True)

    chips = owners // 2

    def cross_ahead(chip):
        return (chip // (chips // 2)) & (chip % 2)

    def cross_back(chip):
        return 1 - cross_ahead((chip + chips - 1) % chips)

    def hop(value, step, cross):
        pairs = []
        for o in range(owners):
            to = (o // 2 + step) % chips
            pairs.append((o, to * 2 + (o % 2 ^ cross(to))))
        return lax.ppermute(value, "owner", pairs)

    def straight(chip):
        return 0

    halves = (block[: groups // 2], block[groups // 2 :])
    back, ahead, far_back, far_ahead = [], [], [], []
    for half in halves:
        back.append(hop(half, 1, straight))
        ahead.append(hop(half, -1, straight))
    for half in range(2):
        far_back.append(hop(back[half], 1, cross_back))
        far_ahead.append(hop(ahead[half], -1, cross_ahead))
    other = lax.ppermute(block, "owner", [(o, o ^ 1) for o in range(owners)])
    far_back[0], far_ahead[0] = lax.optimization_barrier((far_back[0], far_ahead[0]))
    far_back[1], other = lax.optimization_barrier((far_back[1], other))

    chip, core = owner // 2, owner % 2

    def at(d, c):
        return lax.rem(chip + chips + d, chips) * 2 + c

    at_back, at_ahead = at(-1, core), at(1, core)
    at_far_back, at_far_ahead = at(-2, core ^ cross_back(chip)), at(2, core ^ cross_ahead(chip))
    place = jnp.stack(
        [at_ahead, owner, owner ^ 1]
        + [at_far_back, owner, owner ^ 1, at_ahead]
        + [at_far_ahead, at_back, at_far_back]
    )

    def call(kernel, out, slots, scalars, operands, name):
        return pl.pallas_call(
            kernel,
            out_shape=jax.ShapeDtypeStruct(out, jnp.float32),
            scratch_shapes=[
                pltpu.VMEM((slots, groups * MAIN, width), jnp.bfloat16),
                pltpu.VMEM((slots, groups * REM, width), jnp.bfloat16),
                pltpu.VMEM((slots, 1, groups * MAIN), jnp.float32),
                pltpu.VMEM((slots, 1, groups * REM), jnp.float32),
            ],
            in_specs=[smem] * scalars + [vmem] * operands,
            out_specs=vmem,
            compiler_params=params,
            cost_estimate=pl.CostEstimate(flops=1, bytes_accessed=1, transcendentals=0),
            name=name,
        )

    near = call(near_kernel, (8, padded), 3, 0, 4, "near")(block, other, *ahead)
    mid = call(mid_kernel, (8, padded), 4, 0, 6, "mid")(block, other, *ahead, *far_back)
    best = call(late_kernel, (owners, 1, padded), 3, 1, 8, "late")(
        place, near, mid, *back, *far_back, *far_ahead
    )

    best = lax.all_to_all(best, "owner", split_axis=0, concat_axis=0, tiled=True)
    best = jnp.broadcast_to(jnp.max(best, axis=0, keepdims=True), (groups, 1, padded))
    arrived = lax.all_to_all(best, "split", split_axis=0, concat_axis=0, tiled=True)

    result = pl.pallas_call(
        functools.partial(pick_kernel, groups),
        out_shape=jax.ShapeDtypeStruct((1, rows), jnp.float32),
        in_specs=[vmem, vmem, vmem],
        out_specs=vmem,
        compiler_params=params,
        name="pick",
    )(arrived, cluster, slots)
    return result.reshape(rows)


def solution(mesh):
    return jax.shard_map(
        shards,
        mesh=mesh,
        in_specs=(
            P(("rep", "owner", "split"), None),
            P(("rep", "owner", "split")),
            P(("rep", "owner", "split")),
        ),
        out_specs=P(("rep", "owner", "split")),
        check_vma=False,
    )
```

```python
import functools

import jax
import jax.numpy as jnp
from jax import lax
from jax.experimental import pallas as pl
from jax.experimental.pallas import tpu as pltpu
from jax.sharding import PartitionSpec as P

MAIN = 16
REM = 2
RANK_TILE = 8
LANES = 128
ABSENT = 256.0

NT = (((1,), (1,)), ((), ()))
NN = (((1,), (0,)), ((), ()))


def dot(left, right, dims):
    return lax.dot_general(left, right, dims, preferred_element_type=jnp.float32)


def iota(shape, dim):
    return lax.broadcasted_iota(jnp.int32, shape, dim)


def to_column(row):
    parts = []
    for at in range(0, row.shape[1], LANES):
        part = row[:, at : at + LANES]
        n = part.shape[1]
        same = iota((n, n), 0) == iota((n, n), 1)
        parts.append(jnp.sum(jnp.where(same, part, 0.0), axis=1, keepdims=True))
    return jnp.concatenate(parts, axis=0)


def to_row(column):
    parts = []
    for at in range(0, column.shape[0], LANES):
        part = column[at : at + LANES]
        n = part.shape[0]
        same = iota((n, n), 0) == iota((n, n), 1)
        parts.append(jnp.sum(jnp.where(same, part, 0.0), axis=0, keepdims=True))
    return jnp.concatenate(parts, axis=1)


def pack_kernel(groups, home_ref, emb_ref, cluster_ref, rank_ref, out_ref, place_ref):
    rows, width = emb_ref.shape
    pieces = width // LANES
    home = home_ref[0]
    wide = emb_ref[...].astype(jnp.float32)
    norm = jnp.sqrt(jnp.sum(wide * wide, axis=1, keepdims=True) + 1e-06)
    unit = (wide / norm).astype(jnp.bfloat16)

    target = lax.rem(cluster_ref[...], groups)
    target_column = to_column(target.astype(jnp.float32)).astype(jnp.int32)
    earlier = (target_column == target) & (iota((rows, rows), 0) < iota((rows, rows), 1))
    position = jnp.sum(earlier.astype(jnp.float32), axis=0, keepdims=True).astype(jnp.int32)
    is_main = position < MAIN
    place_ref[...] = jnp.where(
        is_main, home * MAIN + position, groups * MAIN + home * REM + position - MAIN
    )

    slot = jnp.where(is_main, target * MAIN + position, -1)
    placing = (iota((groups * MAIN, rows), 0) == slot).astype(jnp.bfloat16)
    main = dot(placing, unit, NN).astype(jnp.bfloat16)
    for k in range(pieces):
        piece = main[:, k * LANES : (k + 1) * LANES]
        out_ref[:, k * MAIN : (k + 1) * MAIN, :] = piece.reshape(groups, MAIN, LANES)

    spread = pieces * REM
    rest = jnp.zeros((groups * spread, LANES), jnp.float32)
    for k in range(pieces):
        slot = jnp.where(is_main, -1, target * spread + k * REM + position - MAIN)
        placing = (iota((groups * spread, rows), 0) == slot).astype(jnp.bfloat16)
        rest += dot(placing, unit[:, k * LANES : (k + 1) * LANES], NN)

    rank = rank_ref[...]
    high = (rank >> 8).astype(jnp.float32) - ABSENT
    low = (rank & 255).astype(jnp.float32)
    line = iota((groups * RANK_TILE, rows), 0)
    mine = line // RANK_TILE == target
    line = line % RANK_TILE
    band = home * MAIN // LANES
    lane = iota((LANES, rows), 0)
    at_main = (lane == jnp.where(is_main, lax.rem(home * MAIN, LANES) + position, -1)).astype(
        jnp.bfloat16
    )
    at_rest = (lane == jnp.where(is_main, -1, home * REM + position - MAIN)).astype(jnp.bfloat16)

    def values(first):
        value = jnp.where(line == first, high, jnp.where(line == first + 1, low, 0.0))
        return jnp.where(mine, value, 0.0).astype(jnp.bfloat16)

    tile = dot(values(2 * band), at_main, NT) + dot(values(4), at_rest, NT)
    shape = (groups * RANK_TILE, LANES)
    line, lane = iota(shape, 0) % RANK_TILE, iota(shape, 1)
    from_main = (line == 2 * band) & (lane // MAIN == lax.rem(home, LANES // MAIN))
    from_rest = (line == 4) & (lane // REM == home)
    tile += jnp.where(from_main | from_rest, ABSENT, 0.0)
    tail = jnp.concatenate(
        [rest.reshape(groups, spread, LANES), tile.reshape(groups, RANK_TILE, LANES)], axis=1
    )
    out_ref[:, pieces * MAIN :, :] = tail.astype(jnp.bfloat16)


def unpack(parts, scratch, slot):
    main_ref, rest_ref, main_rank_ref, rest_rank_ref = scratch
    width = main_ref.shape[2]
    pieces = width // LANES
    mains, rests, spread = main_ref.shape[1], rest_ref.shape[1], pieces * REM
    row, rest, tile = 0, [], 0.0
    for part in parts:
        senders = part.shape[0]
        for k in range(pieces):
            piece = part[:, k * MAIN : (k + 1) * MAIN, :].reshape(senders * MAIN, LANES)
            main_ref[slot, row : row + senders * MAIN, k * LANES : (k + 1) * LANES] = piece
        row += senders * MAIN
        tail = part[:, pieces * MAIN :, :].astype(jnp.float32)
        rest.append(tail[:, :spread, :].reshape(senders * spread, LANES).astype(jnp.bfloat16))
        tile = tile + jnp.sum(tail[:, spread:, :], axis=0)
    rest = jnp.concatenate(rest, axis=0) if len(rest) > 1 else rest[0]
    line, column = iota((pieces * rests, rest.shape[0]), 0), iota((pieces * rests, rest.shape[0]), 1)
    k, line = line // rests, line % rests
    pick = (column == line // REM * spread + k * REM + line % REM).astype(jnp.bfloat16)
    rest = dot(pick, rest, NN).astype(jnp.bfloat16)
    for k in range(pieces):
        rest_ref[slot, :, k * LANES : (k + 1) * LANES] = rest[k * rests : (k + 1) * rests]
    for g in range(mains // LANES):
        high, low = tile[2 * g : 2 * g + 1], tile[2 * g + 1 : 2 * g + 2]
        main_rank_ref[slot, :, g * LANES : (g + 1) * LANES] = high * 256.0 + low
    rest_rank_ref[slot] = (tile[4:5] * 256.0 + tile[5:6])[:, :rests]


def score(query, key, query_rank, key_rank):
    scores = dot(query, key, NT)
    lower = key_rank < query_rank
    return (
        jnp.max(jnp.where(lower, scores, -1.0), axis=1, keepdims=True),
        jnp.max(jnp.where(key_rank > query_rank, scores, -1.0), axis=0, keepdims=True),
    )


def meet(scratch, slots):
    main_ref, rest_ref, main_rank_ref, rest_rank_ref = scratch
    mains, rests, width = main_ref.shape[1], rest_ref.shape[1], main_ref.shape[2]
    others = slots - 1
    other = main_ref[1:slots].reshape(others * mains, width)
    other_rank = jnp.concatenate([to_column(main_rank_ref[i]) for i in range(1, slots)], axis=0)
    rest = rest_ref[0:slots].reshape(slots * rests, width)
    rest_row = jnp.concatenate([rest_rank_ref[i] for i in range(slots)], axis=1)
    rest_rank = to_column(rest_row)
    pivot, pivot_rank = main_ref[0], main_rank_ref[0]
    best_other, best_pivot = score(other, pivot, other_rank, pivot_rank)
    best_rest, found = score(rest, pivot, rest_rank, pivot_rank)
    best_pivot = jnp.maximum(best_pivot, found)
    found, back = score(other, rest_ref[0], other_rank, rest_row[:, :rests])
    best_other = jnp.maximum(best_other, found)
    best_rest = jnp.maximum(best_rest, score(rest, rest, rest_rank, rest_row)[0])
    best_rest = to_row(best_rest)
    results = [(best_pivot, jnp.maximum(best_rest[:, :rests], back))]
    for i in range(others):
        main = to_row(best_other[i * mains : (i + 1) * mains])
        results.append((main, best_rest[:, (i + 1) * rests : (i + 2) * rests]))
    return results


def keep(out_ref, results):
    for i, (main, rest) in enumerate(results):
        n = main.shape[1] + rest.shape[1]
        out_ref[i : i + 1, :n] = jnp.concatenate([main, rest], axis=1)


def near_kernel(own_ref, other_ref, ahead0_ref, ahead1_ref, out_ref, *scratch):
    main_ref, rest_ref, main_rank_ref, rest_rank_ref = scratch
    unpack([ahead0_ref, ahead1_ref], scratch, 0)
    unpack([own_ref], scratch, 1)
    unpack([other_ref], scratch, 2)
    results = meet(scratch, 3)
    rests, width = rest_ref.shape[1], main_ref.shape[2]
    own, own_rank = main_ref[1], to_column(main_rank_ref[1])
    (main_own, rest_own), (main_other, rest_other) = results[1:]
    own_best, _ = score(own, own, own_rank, main_rank_ref[1])
    found, _ = score(own, main_ref[2], own_rank, main_rank_ref[2])
    own_best = to_row(jnp.maximum(own_best, found))
    rest = rest_ref[1:3].reshape(2 * rests, width)
    rest_rank = to_column(jnp.concatenate([rest_rank_ref[1], rest_rank_ref[2]], axis=1))
    found, back = score(rest, own, rest_rank, main_rank_ref[1])
    found = to_row(found)
    main_own = jnp.maximum(jnp.maximum(main_own, own_best), back)
    rest_own = jnp.maximum(rest_own, found[:, :rests])
    found, back = score(rest_ref[1], main_ref[2], rest_rank[:rests], main_rank_ref[2])
    rest_own = jnp.maximum(rest_own, to_row(found))
    keep(out_ref, [results[0], (main_own, rest_own), (main_other, rest_other)])


def mid_kernel(own_ref, other_ref, back0_ref, back1_ref, far_ahead0_ref, far_ahead1_ref, out_ref, *scratch):
    unpack([far_ahead0_ref, far_ahead1_ref], scratch, 0)
    unpack([own_ref], scratch, 1)
    unpack([other_ref], scratch, 2)
    unpack([back0_ref, back1_ref], scratch, 3)
    keep(out_ref, meet(scratch, 4))


def late_kernel(
    place_ref, near_ref, mid_ref, ahead0_ref, ahead1_ref, far_ahead0_ref, far_ahead1_ref, far_back0_ref, far_back1_ref,
    out_ref, *scratch,
):
    unpack([far_back0_ref, far_back1_ref], scratch, 0)
    unpack([ahead0_ref, ahead1_ref], scratch, 1)
    unpack([far_ahead0_ref, far_ahead1_ref], scratch, 2)
    results = meet(scratch, 3)
    mains = results[0][0].shape[1]
    n = mains + results[0][1].shape[1]
    out_ref[...] = jnp.full(out_ref.shape, -1.0, jnp.float32)

    def add(i, values, start, end):
        at = (place_ref[i], slice(None), slice(start, end))
        out_ref[at] = jnp.maximum(out_ref[at], values)

    for i in range(3):
        add(i, near_ref[i : i + 1, :n], 0, n)
    for i in range(4):
        add(3 + i, mid_ref[i : i + 1, :n], 0, n)
    for i, (main, rest) in enumerate(results):
        add(7 + i, main, 0, mains)
        add(7 + i, rest, mains, n)


def pick_kernel(groups, arrived_ref, cluster_ref, place_ref, out_ref):
    arrived = arrived_ref[...].reshape(groups, arrived_ref.shape[2])
    rows = place_ref.shape[1]
    place = (iota((arrived.shape[1], rows), 0) == place_ref[...]).astype(jnp.bfloat16)
    found = jnp.zeros((groups, rows), jnp.float32)
    left = arrived
    for _ in range(3):
        term = left.astype(jnp.bfloat16)
        found += dot(term, place, NN)
        left = left - term.astype(jnp.float32)
    target = lax.rem(cluster_ref[...], groups)
    mine = iota((groups, rows), 0) == target
    out_ref[...] = jnp.sum(jnp.where(mine, found, 0.0), axis=0, keepdims=True)


def shards(embeddings, cluster, rank):
    rows, width = embeddings.shape
    owners, groups = lax.axis_size("owner"), lax.axis_size("split")
    pieces = width // LANES
    depth = pieces * (MAIN + REM) + RANK_TILE
    block_rows = groups * (MAIN + REM)
    padded = -(-block_rows // LANES) * LANES
    owner = lax.axis_index("owner").astype(jnp.int32)
    home = lax.axis_index("split").astype(jnp.int32)
    cluster, rank = cluster.reshape(1, rows), rank.reshape(1, rows)
    smem = pl.BlockSpec(memory_space=pltpu.SMEM)
    vmem = pl.BlockSpec(memory_space=pltpu.VMEM)
    params = pltpu.CompilerParams(vmem_limit_bytes=40 * 1024 * 1024)

    packed, slots = pl.pallas_call(
        functools.partial(pack_kernel, groups),
        out_shape=(
            jax.ShapeDtypeStruct((groups, depth, LANES), jnp.bfloat16),
            jax.ShapeDtypeStruct((1, rows), jnp.int32),
        ),
        in_specs=[smem, vmem, vmem, vmem],
        out_specs=(vmem, vmem),
        compiler_params=params,
        name="pack",
    )(home.reshape(1), embeddings, cluster, rank)

    block = lax.all_to_all(packed, "split", split_axis=0, concat_axis=0, tiled=True)

    chips = owners // 2

    def cross_ahead(chip):
        return (chip // (chips // 2)) & (chip % 2)

    def cross_back(chip):
        return 1 - cross_ahead((chip + chips - 1) % chips)

    def hop(value, step, cross):
        pairs = []
        for o in range(owners):
            to = (o // 2 + step) % chips
            pairs.append((o, to * 2 + (o % 2 ^ cross(to))))
        return lax.ppermute(value, "owner", pairs)

    def straight(chip):
        return 0

    large = groups * 10 // 16
    halves = (block[:large], block[large:])
    back, ahead, far_back, far_ahead = [], [], [], []
    for half in halves:
        back.append(hop(half, 1, straight))
        ahead.append(hop(half, -1, straight))
    for half in range(2):
        far_back.append(hop(back[half], 1, cross_back))
        far_ahead.append(hop(ahead[half], -1, cross_ahead))
    other = lax.ppermute(block, "owner", [(o, o ^ 1) for o in range(owners)])
    far_back[0], far_ahead[0] = lax.optimization_barrier((far_back[0], far_ahead[0]))

    chip, core = owner // 2, owner % 2

    def at(d, c):
        return lax.rem(chip + chips + d, chips) * 2 + c

    at_back, at_ahead = at(-1, core), at(1, core)
    at_far_back, at_far_ahead = at(-2, core ^ cross_back(chip)), at(2, core ^ cross_ahead(chip))
    place = jnp.stack(
        [at_ahead, owner, owner ^ 1]
        + [at_far_ahead, owner, owner ^ 1, at_back]
        + [at_far_back, at_ahead, at_far_ahead]
    )

    def call(kernel, out, slots, scalars, operands, name):
        return pl.pallas_call(
            kernel,
            out_shape=jax.ShapeDtypeStruct(out, jnp.float32),
            scratch_shapes=[
                pltpu.VMEM((slots, groups * MAIN, width), jnp.bfloat16),
                pltpu.VMEM((slots, groups * REM, width), jnp.bfloat16),
                pltpu.VMEM((slots, 1, groups * MAIN), jnp.float32),
                pltpu.VMEM((slots, 1, groups * REM), jnp.float32),
            ],
            in_specs=[smem] * scalars + [vmem] * operands,
            out_specs=vmem,
            compiler_params=params,
            cost_estimate=pl.CostEstimate(flops=1, bytes_accessed=1, transcendentals=0),
            name=name,
        )

    near = call(near_kernel, (8, padded), 3, 0, 4, "near")(block, other, *ahead)
    mid = call(mid_kernel, (8, padded), 4, 0, 6, "mid")(block, other, *back, *far_ahead)
    best = call(late_kernel, (owners, 1, padded), 3, 1, 8, "late")(
        place, near, mid, *ahead, *far_ahead, *far_back
    )

    best = lax.all_to_all(best, "owner", split_axis=0, concat_axis=0, tiled=True)
    best = jnp.broadcast_to(jnp.max(best, axis=0, keepdims=True), (groups, 1, padded))
    arrived = lax.all_to_all(best, "split", split_axis=0, concat_axis=0, tiled=True)

    result = pl.pallas_call(
        functools.partial(pick_kernel, groups),
        out_shape=jax.ShapeDtypeStruct((1, rows), jnp.float32),
        in_specs=[vmem, vmem, vmem],
        out_specs=vmem,
        compiler_params=params,
        name="pick",
    )(arrived, cluster, slots)
    return result.reshape(rows)


def solution(mesh):
    return jax.shard_map(
        shards,
        mesh=mesh,
        in_specs=(
            P(("rep", "owner", "split"), None),
            P(("rep", "owner", "split")),
            P(("rep", "owner", "split")),
        ),
        out_specs=P(("rep", "owner", "split")),
        check_vma=False,
    )
```

```python
import functools

import jax
import jax.numpy as jnp
from jax import lax
from jax.experimental import pallas as pl
from jax.experimental.pallas import tpu as pltpu
from jax.sharding import PartitionSpec as P

MAIN = 16
REM = 2
RANK_TILE = 8
LANES = 128
ABSENT = 256.0

NT = (((1,), (1,)), ((), ()))
NN = (((1,), (0,)), ((), ()))


def dot(left, right, dims):
    return lax.dot_general(left, right, dims, preferred_element_type=jnp.float32)


def iota(shape, dim):
    return lax.broadcasted_iota(jnp.int32, shape, dim)


def to_column(row):
    parts = []
    for at in range(0, row.shape[1], LANES):
        part = row[:, at : at + LANES]
        n = part.shape[1]
        same = iota((n, n), 0) == iota((n, n), 1)
        parts.append(jnp.sum(jnp.where(same, part, 0.0), axis=1, keepdims=True))
    return jnp.concatenate(parts, axis=0)


def to_row(column):
    parts = []
    for at in range(0, column.shape[0], LANES):
        part = column[at : at + LANES]
        n = part.shape[0]
        same = iota((n, n), 0) == iota((n, n), 1)
        parts.append(jnp.sum(jnp.where(same, part, 0.0), axis=0, keepdims=True))
    return jnp.concatenate(parts, axis=1)


def pack_kernel(groups, home_ref, emb_ref, cluster_ref, rank_ref, out_ref, place_ref):
    rows, width = emb_ref.shape
    pieces = width // LANES
    home = home_ref[0]
    wide = emb_ref[...].astype(jnp.float32)
    norm = jnp.sqrt(jnp.sum(wide * wide, axis=1, keepdims=True) + 1e-06)
    unit = (wide / norm).astype(jnp.bfloat16)

    target = lax.rem(cluster_ref[...], groups)
    target_column = to_column(target.astype(jnp.float32)).astype(jnp.int32)
    earlier = (target_column == target) & (iota((rows, rows), 0) < iota((rows, rows), 1))
    position = jnp.sum(earlier.astype(jnp.float32), axis=0, keepdims=True).astype(jnp.int32)
    is_main = position < MAIN
    place_ref[...] = jnp.where(
        is_main, home * MAIN + position, groups * MAIN + home * REM + position - MAIN
    )

    slot = jnp.where(is_main, target * MAIN + position, -1)
    placing = (iota((groups * MAIN, rows), 0) == slot).astype(jnp.bfloat16)
    main = dot(placing, unit, NN).astype(jnp.bfloat16)
    for k in range(pieces):
        piece = main[:, k * LANES : (k + 1) * LANES]
        out_ref[:, k * MAIN : (k + 1) * MAIN, :] = piece.reshape(groups, MAIN, LANES)

    spread = pieces * REM
    rest = jnp.zeros((groups * spread, LANES), jnp.float32)
    for k in range(pieces):
        slot = jnp.where(is_main, -1, target * spread + k * REM + position - MAIN)
        placing = (iota((groups * spread, rows), 0) == slot).astype(jnp.bfloat16)
        rest += dot(placing, unit[:, k * LANES : (k + 1) * LANES], NN)

    rank = rank_ref[...]
    high = (rank >> 8).astype(jnp.float32) - ABSENT
    low = (rank & 255).astype(jnp.float32)
    line = iota((groups * RANK_TILE, rows), 0)
    mine = line // RANK_TILE == target
    line = line % RANK_TILE
    band = home * MAIN // LANES
    lane = iota((LANES, rows), 0)
    at_main = (lane == jnp.where(is_main, lax.rem(home * MAIN, LANES) + position, -1)).astype(
        jnp.bfloat16
    )
    at_rest = (lane == jnp.where(is_main, -1, home * REM + position - MAIN)).astype(jnp.bfloat16)

    def values(first):
        value = jnp.where(line == first, high, jnp.where(line == first + 1, low, 0.0))
        return jnp.where(mine, value, 0.0).astype(jnp.bfloat16)

    tile = dot(values(2 * band), at_main, NT) + dot(values(4), at_rest, NT)
    shape = (groups * RANK_TILE, LANES)
    line, lane = iota(shape, 0) % RANK_TILE, iota(shape, 1)
    from_main = (line == 2 * band) & (lane // MAIN == lax.rem(home, LANES // MAIN))
    from_rest = (line == 4) & (lane // REM == home)
    tile += jnp.where(from_main | from_rest, ABSENT, 0.0)
    tail = jnp.concatenate(
        [rest.reshape(groups, spread, LANES), tile.reshape(groups, RANK_TILE, LANES)], axis=1
    )
    out_ref[:, pieces * MAIN :, :] = tail.astype(jnp.bfloat16)


def unpack(parts, scratch, slot):
    main_ref, rest_ref, main_rank_ref, rest_rank_ref = scratch
    width = main_ref.shape[2]
    pieces = width // LANES
    mains, rests, spread = main_ref.shape[1], rest_ref.shape[1], pieces * REM
    row, rest, tile = 0, [], 0.0
    for part in parts:
        senders = part.shape[0]
        for k in range(pieces):
            piece = part[:, k * MAIN : (k + 1) * MAIN, :].reshape(senders * MAIN, LANES)
            main_ref[slot, row : row + senders * MAIN, k * LANES : (k + 1) * LANES] = piece
        row += senders * MAIN
        tail = part[:, pieces * MAIN :, :].astype(jnp.float32)
        rest.append(tail[:, :spread, :].reshape(senders * spread, LANES).astype(jnp.bfloat16))
        tile = tile + jnp.sum(tail[:, spread:, :], axis=0)
    rest = jnp.concatenate(rest, axis=0) if len(rest) > 1 else rest[0]
    line, column = iota((pieces * rests, rest.shape[0]), 0), iota((pieces * rests, rest.shape[0]), 1)
    k, line = line // rests, line % rests
    pick = (column == line // REM * spread + k * REM + line % REM).astype(jnp.bfloat16)
    rest = dot(pick, rest, NN).astype(jnp.bfloat16)
    for k in range(pieces):
        rest_ref[slot, :, k * LANES : (k + 1) * LANES] = rest[k * rests : (k + 1) * rests]
    for g in range(mains // LANES):
        high, low = tile[2 * g : 2 * g + 1], tile[2 * g + 1 : 2 * g + 2]
        main_rank_ref[slot, :, g * LANES : (g + 1) * LANES] = high * 256.0 + low
    rest_rank_ref[slot] = (tile[4:5] * 256.0 + tile[5:6])[:, :rests]


def score(query, key, query_rank, key_rank):
    scores = dot(query, key, NT)
    lower = key_rank < query_rank
    return (
        jnp.max(jnp.where(lower, scores, -1.0), axis=1, keepdims=True),
        jnp.max(jnp.where(key_rank > query_rank, scores, -1.0), axis=0, keepdims=True),
    )


def meet(scratch, slots):
    main_ref, rest_ref, main_rank_ref, rest_rank_ref = scratch
    mains, rests, width = main_ref.shape[1], rest_ref.shape[1], main_ref.shape[2]
    others = slots - 1
    other = main_ref[1:slots].reshape(others * mains, width)
    other_rank = jnp.concatenate([to_column(main_rank_ref[i]) for i in range(1, slots)], axis=0)
    rest = rest_ref[0:slots].reshape(slots * rests, width)
    rest_row = jnp.concatenate([rest_rank_ref[i] for i in range(slots)], axis=1)
    rest_rank = to_column(rest_row)
    pivot, pivot_rank = main_ref[0], main_rank_ref[0]
    best_other, best_pivot = score(other, pivot, other_rank, pivot_rank)
    best_rest, found = score(rest, pivot, rest_rank, pivot_rank)
    best_pivot = jnp.maximum(best_pivot, found)
    found, back = score(other, rest_ref[0], other_rank, rest_row[:, :rests])
    best_other = jnp.maximum(best_other, found)
    best_rest = jnp.maximum(best_rest, score(rest, rest, rest_rank, rest_row)[0])
    best_rest = to_row(best_rest)
    results = [(best_pivot, jnp.maximum(best_rest[:, :rests], back))]
    for i in range(others):
        main = to_row(best_other[i * mains : (i + 1) * mains])
        results.append((main, best_rest[:, (i + 1) * rests : (i + 2) * rests]))
    return results


def keep(out_ref, results):
    for i, (main, rest) in enumerate(results):
        n = main.shape[1] + rest.shape[1]
        out_ref[i : i + 1, :n] = jnp.concatenate([main, rest], axis=1)


def near_kernel(own_ref, other_ref, ahead0_ref, ahead1_ref, out_ref, *scratch):
    main_ref, rest_ref, main_rank_ref, rest_rank_ref = scratch
    unpack([ahead0_ref, ahead1_ref], scratch, 0)
    unpack([own_ref], scratch, 1)
    unpack([other_ref], scratch, 2)
    results = meet(scratch, 3)
    rests, width = rest_ref.shape[1], main_ref.shape[2]
    own, own_rank = main_ref[1], to_column(main_rank_ref[1])
    (main_own, rest_own), (main_other, rest_other) = results[1:]
    own_best, _ = score(own, own, own_rank, main_rank_ref[1])
    found, _ = score(own, main_ref[2], own_rank, main_rank_ref[2])
    own_best = to_row(jnp.maximum(own_best, found))
    rest = rest_ref[1:3].reshape(2 * rests, width)
    rest_rank = to_column(jnp.concatenate([rest_rank_ref[1], rest_rank_ref[2]], axis=1))
    found, back = score(rest, own, rest_rank, main_rank_ref[1])
    found = to_row(found)
    main_own = jnp.maximum(jnp.maximum(main_own, own_best), back)
    rest_own = jnp.maximum(rest_own, found[:, :rests])
    found, back = score(rest_ref[1], main_ref[2], rest_rank[:rests], main_rank_ref[2])
    rest_own = jnp.maximum(rest_own, to_row(found))
    keep(out_ref, [results[0], (main_own, rest_own), (main_other, rest_other)])


def mid_kernel(own_ref, other_ref, ahead0_ref, ahead1_ref, back0_ref, back1_ref, out_ref, *scratch):
    unpack([back0_ref, back1_ref], scratch, 0)
    unpack([own_ref], scratch, 1)
    unpack([other_ref], scratch, 2)
    unpack([ahead0_ref, ahead1_ref], scratch, 3)
    keep(out_ref, meet(scratch, 4))


def late_kernel(
    place_ref, near_ref, mid_ref, back0_ref, back1_ref, far_back0_ref, far_back1_ref, far_ahead0_ref, far_ahead1_ref,
    out_ref, *scratch,
):
    unpack([back0_ref, back1_ref], scratch, 1)
    unpack([far_back0_ref, far_back1_ref], scratch, 2)
    unpack([far_ahead0_ref, far_ahead1_ref], scratch, 0)
    results = meet(scratch, 3)
    mains = results[0][0].shape[1]
    n = mains + results[0][1].shape[1]
    out_ref[...] = jnp.full(out_ref.shape, -1.0, jnp.float32)

    def add(i, values, start, end):
        at = (place_ref[i], slice(None), slice(start, end))
        out_ref[at] = jnp.maximum(out_ref[at], values)

    for i in range(3):
        add(i, near_ref[i : i + 1, :n], 0, n)
    for i in range(4):
        add(3 + i, mid_ref[i : i + 1, :n], 0, n)
    for i, (main, rest) in enumerate(results):
        add(7 + i, main, 0, mains)
        add(7 + i, rest, mains, n)


def pick_kernel(groups, arrived_ref, cluster_ref, place_ref, out_ref):
    arrived = arrived_ref[...].reshape(groups, arrived_ref.shape[2])
    rows = place_ref.shape[1]
    place = (iota((arrived.shape[1], rows), 0) == place_ref[...]).astype(jnp.bfloat16)
    found = jnp.zeros((groups, rows), jnp.float32)
    left = arrived
    for _ in range(3):
        term = left.astype(jnp.bfloat16)
        found += dot(term, place, NN)
        left = left - term.astype(jnp.float32)
    target = lax.rem(cluster_ref[...], groups)
    mine = iota((groups, rows), 0) == target
    out_ref[...] = jnp.sum(jnp.where(mine, found, 0.0), axis=0, keepdims=True)


def shards(embeddings, cluster, rank):
    rows, width = embeddings.shape
    owners, groups = lax.axis_size("owner"), lax.axis_size("split")
    pieces = width // LANES
    depth = pieces * (MAIN + REM) + RANK_TILE
    block_rows = groups * (MAIN + REM)
    padded = -(-block_rows // LANES) * LANES
    owner = lax.axis_index("owner").astype(jnp.int32)
    home = lax.axis_index("split").astype(jnp.int32)
    cluster, rank = cluster.reshape(1, rows), rank.reshape(1, rows)
    smem = pl.BlockSpec(memory_space=pltpu.SMEM)
    vmem = pl.BlockSpec(memory_space=pltpu.VMEM)
    params = pltpu.CompilerParams(vmem_limit_bytes=40 * 1024 * 1024)

    packed, slots = pl.pallas_call(
        functools.partial(pack_kernel, groups),
        out_shape=(
            jax.ShapeDtypeStruct((groups, depth, LANES), jnp.bfloat16),
            jax.ShapeDtypeStruct((1, rows), jnp.int32),
        ),
        in_specs=[smem, vmem, vmem, vmem],
        out_specs=(vmem, vmem),
        compiler_params=params,
        name="pack",
    )(home.reshape(1), embeddings, cluster, rank)

    block = lax.all_to_all(packed, "split", split_axis=0, concat_axis=0, tiled=True)

    chips = owners // 2

    def cross_ahead(chip):
        return (chip // (chips // 2)) & (chip % 2)

    def cross_back(chip):
        return 1 - cross_ahead((chip + chips - 1) % chips)

    def hop(value, step, cross):
        pairs = []
        for o in range(owners):
            to = (o // 2 + step) % chips
            pairs.append((o, to * 2 + (o % 2 ^ cross(to))))
        return lax.ppermute(value, "owner", pairs)

    def straight(chip):
        return 0

    def cut(large):
        return block[:large], block[large:]

    back = [hop(part, 1, straight) for part in cut(groups * 10 // 16)]
    ahead = [hop(part, -1, straight) for part in cut(groups * 9 // 16)]
    far_back = [hop(part, 1, cross_back) for part in back]
    far_ahead = [hop(part, -1, cross_ahead) for part in ahead]
    other = lax.ppermute(block, "owner", [(o, o ^ 1) for o in range(owners)])
    far_back[0], far_ahead[0] = lax.optimization_barrier((far_back[0], far_ahead[0]))

    chip, core = owner // 2, owner % 2

    def at(d, c):
        return lax.rem(chip + chips + d, chips) * 2 + c

    at_back, at_ahead = at(-1, core), at(1, core)
    at_far_back, at_far_ahead = at(-2, core ^ cross_back(chip)), at(2, core ^ cross_ahead(chip))
    place = jnp.stack(
        [at_ahead, owner, owner ^ 1]
        + [at_far_back, owner, owner ^ 1, at_ahead]
        + [at_far_ahead, at_back, at_far_back]
    )

    def call(kernel, out, slots, scalars, operands, name):
        return pl.pallas_call(
            kernel,
            out_shape=jax.ShapeDtypeStruct(out, jnp.float32),
            scratch_shapes=[
                pltpu.VMEM((slots, groups * MAIN, width), jnp.bfloat16),
                pltpu.VMEM((slots, groups * REM, width), jnp.bfloat16),
                pltpu.VMEM((slots, 1, groups * MAIN), jnp.float32),
                pltpu.VMEM((slots, 1, groups * REM), jnp.float32),
            ],
            in_specs=[smem] * scalars + [vmem] * operands,
            out_specs=vmem,
            compiler_params=params,
            cost_estimate=pl.CostEstimate(flops=1, bytes_accessed=1, transcendentals=0),
            name=name,
        )

    near = call(near_kernel, (8, padded), 3, 0, 4, "near")(block, other, *ahead)
    mid = call(mid_kernel, (8, padded), 4, 0, 6, "mid")(block, other, *ahead, *far_back)
    best = call(late_kernel, (owners, 1, padded), 3, 1, 8, "late")(
        place, near, mid, *back, *far_back, *far_ahead
    )

    best = lax.all_to_all(best, "owner", split_axis=0, concat_axis=0, tiled=True)
    best = jnp.broadcast_to(jnp.max(best, axis=0, keepdims=True), (groups, 1, padded))
    arrived = lax.all_to_all(best, "split", split_axis=0, concat_axis=0, tiled=True)

    result = pl.pallas_call(
        functools.partial(pick_kernel, groups),
        out_shape=jax.ShapeDtypeStruct((1, rows), jnp.float32),
        in_specs=[vmem, vmem, vmem],
        out_specs=vmem,
        compiler_params=params,
        name="pick",
    )(arrived, cluster, slots)
    return result.reshape(rows)


def solution(mesh):
    return jax.shard_map(
        shards,
        mesh=mesh,
        in_specs=(
            P(("rep", "owner", "split"), None),
            P(("rep", "owner", "split")),
            P(("rep", "owner", "split")),
        ),
        out_specs=P(("rep", "owner", "split")),
        check_vma=False,
    )
```

```python
import functools

import jax
import jax.numpy as jnp
from jax import lax
from jax.experimental import pallas as pl
from jax.experimental.pallas import tpu as pltpu
from jax.sharding import PartitionSpec as P

MAIN = 16
REM = 2
RANK_TILE = 8
LANES = 128
ABSENT = 256.0

NT = (((1,), (1,)), ((), ()))
NN = (((1,), (0,)), ((), ()))


def dot(left, right, dims):
    return lax.dot_general(left, right, dims, preferred_element_type=jnp.float32)


def iota(shape, dim):
    return lax.broadcasted_iota(jnp.int32, shape, dim)


def to_column(row):
    parts = []
    for at in range(0, row.shape[1], LANES):
        part = row[:, at : at + LANES]
        n = part.shape[1]
        same = iota((n, n), 0) == iota((n, n), 1)
        parts.append(jnp.sum(jnp.where(same, part, 0.0), axis=1, keepdims=True))
    return jnp.concatenate(parts, axis=0)


def to_row(column):
    parts = []
    for at in range(0, column.shape[0], LANES):
        part = column[at : at + LANES]
        n = part.shape[0]
        same = iota((n, n), 0) == iota((n, n), 1)
        parts.append(jnp.sum(jnp.where(same, part, 0.0), axis=0, keepdims=True))
    return jnp.concatenate(parts, axis=1)


def pack_kernel(groups, home_ref, emb_ref, cluster_ref, rank_ref, out_ref, place_ref):
    rows, width = emb_ref.shape
    pieces = width // LANES
    home = home_ref[0]
    wide = emb_ref[...].astype(jnp.float32)
    norm = jnp.sqrt(jnp.sum(wide * wide, axis=1, keepdims=True) + 1e-06)
    unit = (wide / norm).astype(jnp.bfloat16)

    target = lax.rem(cluster_ref[...], groups)
    target_column = to_column(target.astype(jnp.float32)).astype(jnp.int32)
    earlier = (target_column == target) & (iota((rows, rows), 0) < iota((rows, rows), 1))
    position = jnp.sum(earlier.astype(jnp.float32), axis=0, keepdims=True).astype(jnp.int32)
    is_main = position < MAIN
    place_ref[...] = jnp.where(
        is_main, home * MAIN + position, groups * MAIN + home * REM + position - MAIN
    )

    slot = jnp.where(is_main, target * MAIN + position, -1)
    placing = (iota((groups * MAIN, rows), 0) == slot).astype(jnp.bfloat16)
    main = dot(placing, unit, NN).astype(jnp.bfloat16)
    for k in range(pieces):
        piece = main[:, k * LANES : (k + 1) * LANES]
        out_ref[:, k * MAIN : (k + 1) * MAIN, :] = piece.reshape(groups, MAIN, LANES)

    spread = pieces * REM
    rest = jnp.zeros((groups * spread, LANES), jnp.float32)
    for k in range(pieces):
        slot = jnp.where(is_main, -1, target * spread + k * REM + position - MAIN)
        placing = (iota((groups * spread, rows), 0) == slot).astype(jnp.bfloat16)
        rest += dot(placing, unit[:, k * LANES : (k + 1) * LANES], NN)

    rank = rank_ref[...]
    high = (rank >> 8).astype(jnp.float32) - ABSENT
    low = (rank & 255).astype(jnp.float32)
    line = iota((groups * RANK_TILE, rows), 0)
    mine = line // RANK_TILE == target
    line = line % RANK_TILE
    band = home * MAIN // LANES
    lane = iota((LANES, rows), 0)
    at_main = (lane == jnp.where(is_main, lax.rem(home * MAIN, LANES) + position, -1)).astype(
        jnp.bfloat16
    )
    at_rest = (lane == jnp.where(is_main, -1, home * REM + position - MAIN)).astype(jnp.bfloat16)

    def values(first):
        value = jnp.where(line == first, high, jnp.where(line == first + 1, low, 0.0))
        return jnp.where(mine, value, 0.0).astype(jnp.bfloat16)

    tile = dot(values(2 * band), at_main, NT) + dot(values(4), at_rest, NT)
    shape = (groups * RANK_TILE, LANES)
    line, lane = iota(shape, 0) % RANK_TILE, iota(shape, 1)
    from_main = (line == 2 * band) & (lane // MAIN == lax.rem(home, LANES // MAIN))
    from_rest = (line == 4) & (lane // REM == home)
    tile += jnp.where(from_main | from_rest, ABSENT, 0.0)
    tail = jnp.concatenate(
        [rest.reshape(groups, spread, LANES), tile.reshape(groups, RANK_TILE, LANES)], axis=1
    )
    out_ref[:, pieces * MAIN :, :] = tail.astype(jnp.bfloat16)


def unpack(parts, scratch, slot):
    main_ref, rest_ref, main_rank_ref, rest_rank_ref = scratch
    width = main_ref.shape[2]
    pieces = width // LANES
    mains, rests, spread = main_ref.shape[1], rest_ref.shape[1], pieces * REM
    row, rest, tile = 0, [], 0.0
    for part in parts:
        senders = part.shape[0]
        for k in range(pieces):
            piece = part[:, k * MAIN : (k + 1) * MAIN, :].reshape(senders * MAIN, LANES)
            main_ref[slot, row : row + senders * MAIN, k * LANES : (k + 1) * LANES] = piece
        row += senders * MAIN
        tail = part[:, pieces * MAIN :, :].astype(jnp.float32)
        rest.append(tail[:, :spread, :].reshape(senders * spread, LANES).astype(jnp.bfloat16))
        tile = tile + jnp.sum(tail[:, spread:, :], axis=0)
    rest = jnp.concatenate(rest, axis=0) if len(rest) > 1 else rest[0]
    line, column = iota((pieces * rests, rest.shape[0]), 0), iota((pieces * rests, rest.shape[0]), 1)
    k, line = line // rests, line % rests
    pick = (column == line // REM * spread + k * REM + line % REM).astype(jnp.bfloat16)
    rest = dot(pick, rest, NN).astype(jnp.bfloat16)
    for k in range(pieces):
        rest_ref[slot, :, k * LANES : (k + 1) * LANES] = rest[k * rests : (k + 1) * rests]
    for g in range(mains // LANES):
        high, low = tile[2 * g : 2 * g + 1], tile[2 * g + 1 : 2 * g + 2]
        main_rank_ref[slot, :, g * LANES : (g + 1) * LANES] = high * 256.0 + low
    rest_rank_ref[slot] = (tile[4:5] * 256.0 + tile[5:6])[:, :rests]


def score(query, key, query_rank, key_rank):
    scores = dot(query, key, NT)
    lower = key_rank < query_rank
    return (
        jnp.max(jnp.where(lower, scores, -1.0), axis=1, keepdims=True),
        jnp.max(jnp.where(lower, -1.0, scores), axis=0, keepdims=True),
    )


def meet(scratch, slots):
    main_ref, rest_ref, main_rank_ref, rest_rank_ref = scratch
    mains, rests, width = main_ref.shape[1], rest_ref.shape[1], main_ref.shape[2]
    others = slots - 1
    other = main_ref[1:slots].reshape(others * mains, width)
    other_rank = jnp.concatenate([to_column(main_rank_ref[i]) for i in range(1, slots)], axis=0)
    rest = rest_ref[0:slots].reshape(slots * rests, width)
    rest_row = jnp.concatenate([rest_rank_ref[i] for i in range(slots)], axis=1)
    rest_rank = to_column(rest_row)
    pivot, pivot_rank = main_ref[0], main_rank_ref[0]
    best_other, best_pivot = score(other, pivot, other_rank, pivot_rank)
    best_rest, found = score(rest, pivot, rest_rank, pivot_rank)
    best_pivot = jnp.maximum(best_pivot, found)
    found, back = score(other, rest_ref[0], other_rank, rest_row[:, :rests])
    best_other = jnp.maximum(best_other, found)
    best_rest = jnp.maximum(best_rest, score(rest, rest, rest_rank, rest_row)[0])
    best_rest = to_row(best_rest)
    results = [(best_pivot, jnp.maximum(best_rest[:, :rests], back))]
    for i in range(others):
        main = to_row(best_other[i * mains : (i + 1) * mains])
        results.append((main, best_rest[:, (i + 1) * rests : (i + 2) * rests]))
    return results


def keep(out_ref, results):
    for i, (main, rest) in enumerate(results):
        n = main.shape[1] + rest.shape[1]
        out_ref[i : i + 1, :n] = jnp.concatenate([main, rest], axis=1)


def near_kernel(own_ref, other_ref, ahead0_ref, ahead1_ref, out_ref, *scratch):
    main_ref, rest_ref, main_rank_ref, rest_rank_ref = scratch
    unpack([ahead0_ref, ahead1_ref], scratch, 0)
    unpack([own_ref], scratch, 1)
    unpack([other_ref], scratch, 2)
    results = meet(scratch, 3)
    rests, width = rest_ref.shape[1], main_ref.shape[2]
    own, own_rank = main_ref[1], to_column(main_rank_ref[1])
    (main_own, rest_own), (main_other, rest_other) = results[1:]
    own_best, _ = score(own, own, own_rank, main_rank_ref[1])
    found, _ = score(own, main_ref[2], own_rank, main_rank_ref[2])
    own_best = to_row(jnp.maximum(own_best, found))
    rest = rest_ref[1:3].reshape(2 * rests, width)
    rest_rank = to_column(jnp.concatenate([rest_rank_ref[1], rest_rank_ref[2]], axis=1))
    found, back = score(rest, own, rest_rank, main_rank_ref[1])
    found = to_row(found)
    main_own = jnp.maximum(jnp.maximum(main_own, own_best), back)
    rest_own = jnp.maximum(rest_own, found[:, :rests])
    found, back = score(rest_ref[1], main_ref[2], rest_rank[:rests], main_rank_ref[2])
    rest_own = jnp.maximum(rest_own, to_row(found))
    keep(out_ref, [results[0], (main_own, rest_own), (main_other, rest_other)])


def mid_kernel(own_ref, other_ref, ahead0_ref, ahead1_ref, back0_ref, back1_ref, out_ref, *scratch):
    unpack([back0_ref, back1_ref], scratch, 0)
    unpack([own_ref], scratch, 1)
    unpack([other_ref], scratch, 2)
    unpack([ahead0_ref, ahead1_ref], scratch, 3)
    keep(out_ref, meet(scratch, 4))


def late_kernel(
    place_ref, near_ref, mid_ref, back0_ref, back1_ref, far_back0_ref, far_back1_ref, far_ahead0_ref, far_ahead1_ref,
    out_ref, *scratch,
):
    main_ref, rest_ref, _, _ = scratch
    unpack([back0_ref, back1_ref], scratch, 1)
    unpack([far_back0_ref, far_back1_ref], scratch, 2)
    unpack([far_ahead0_ref, far_ahead1_ref], scratch, 0)
    mains = main_ref.shape[1]
    n = mains + rest_ref.shape[1]
    out_ref[...] = jnp.full(out_ref.shape, -1.0, jnp.float32)

    def add(i, values, start, end):
        at = (place_ref[i], slice(None), slice(start, end))
        out_ref[at] = jnp.maximum(out_ref[at], values)

    for i in range(3):
        add(i, near_ref[i : i + 1, :n], 0, n)
    for i in range(4):
        add(3 + i, mid_ref[i : i + 1, :n], 0, n)
    for i, (main, rest) in enumerate(meet(scratch, 3)):
        add(7 + i, main, 0, mains)
        add(7 + i, rest, mains, n)


def pick_kernel(groups, arrived_ref, cluster_ref, place_ref, out_ref):
    arrived = arrived_ref[...].reshape(groups, arrived_ref.shape[2])
    rows = place_ref.shape[1]
    place = (iota((arrived.shape[1], rows), 0) == place_ref[...]).astype(jnp.bfloat16)
    found = jnp.zeros((groups, rows), jnp.float32)
    left = arrived
    for _ in range(3):
        term = left.astype(jnp.bfloat16)
        found += dot(term, place, NN)
        left = left - term.astype(jnp.float32)
    target = lax.rem(cluster_ref[...], groups)
    mine = iota((groups, rows), 0) == target
    out_ref[...] = jnp.sum(jnp.where(mine, found, 0.0), axis=0, keepdims=True)


def shards(embeddings, cluster, rank):
    rows, width = embeddings.shape
    owners, groups = lax.axis_size("owner"), lax.axis_size("split")
    pieces = width // LANES
    depth = pieces * (MAIN + REM) + RANK_TILE
    block_rows = groups * (MAIN + REM)
    padded = -(-block_rows // LANES) * LANES
    owner = lax.axis_index("owner").astype(jnp.int32)
    home = lax.axis_index("split").astype(jnp.int32)
    cluster, rank = cluster.reshape(1, rows), rank.reshape(1, rows)
    smem = pl.BlockSpec(memory_space=pltpu.SMEM)
    vmem = pl.BlockSpec(memory_space=pltpu.VMEM)
    params = pltpu.CompilerParams(vmem_limit_bytes=40 * 1024 * 1024)

    packed, slots = pl.pallas_call(
        functools.partial(pack_kernel, groups),
        out_shape=(
            jax.ShapeDtypeStruct((groups, depth, LANES), jnp.bfloat16),
            jax.ShapeDtypeStruct((1, rows), jnp.int32),
        ),
        in_specs=[smem, vmem, vmem, vmem],
        out_specs=(vmem, vmem),
        compiler_params=params,
        name="pack",
    )(home.reshape(1), embeddings, cluster, rank)

    block = lax.all_to_all(packed, "split", split_axis=0, concat_axis=0, tiled=True)

    chips = owners // 2

    def cross_ahead(chip):
        return (chip // (chips // 2)) & (chip % 2)

    def cross_back(chip):
        return 1 - cross_ahead((chip + chips - 1) % chips)

    def hop(value, step, cross):
        pairs = []
        for o in range(owners):
            to = (o // 2 + step) % chips
            pairs.append((o, to * 2 + (o % 2 ^ cross(to))))
        return lax.ppermute(value, "owner", pairs)

    def straight(chip):
        return 0

    def cut(large):
        return block[:large], block[large:]

    back = [hop(part, 1, straight) for part in cut(groups * 10 // 16)]
    ahead = [hop(part, -1, straight) for part in cut(groups * 9 // 16)]
    far_back = [hop(part, 1, cross_back) for part in back]
    far_ahead = [hop(part, -1, cross_ahead) for part in ahead]
    other = lax.ppermute(block, "owner", [(o, o ^ 1) for o in range(owners)])
    far_back[0], far_ahead[0] = lax.optimization_barrier((far_back[0], far_ahead[0]))

    chip, core = owner // 2, owner % 2

    def at(d, c):
        return lax.rem(chip + chips + d, chips) * 2 + c

    at_back, at_ahead = at(-1, core), at(1, core)
    at_far_back, at_far_ahead = at(-2, core ^ cross_back(chip)), at(2, core ^ cross_ahead(chip))
    place = jnp.stack(
        [at_ahead, owner, owner ^ 1]
        + [at_far_back, owner, owner ^ 1, at_ahead]
        + [at_far_ahead, at_back, at_far_back]
    )

    def call(kernel, out, slots, scalars, operands, name):
        return pl.pallas_call(
            kernel,
            out_shape=jax.ShapeDtypeStruct(out, jnp.float32),
            scratch_shapes=[
                pltpu.VMEM((slots, groups * MAIN, width), jnp.bfloat16),
                pltpu.VMEM((slots, groups * REM, width), jnp.bfloat16),
                pltpu.VMEM((slots, 1, groups * MAIN), jnp.float32),
                pltpu.VMEM((slots, 1, groups * REM), jnp.float32),
            ],
            in_specs=[smem] * scalars + [vmem] * operands,
            out_specs=vmem,
            compiler_params=params,
            cost_estimate=pl.CostEstimate(flops=1, bytes_accessed=1, transcendentals=0),
            name=name,
        )

    near = call(near_kernel, (8, padded), 3, 0, 4, "near")(block, other, *ahead)
    mid = call(mid_kernel, (8, padded), 4, 0, 6, "mid")(block, other, *ahead, *far_back)
    best = call(late_kernel, (owners, 1, padded), 3, 1, 8, "late")(
        place, near, mid, *back, *far_back, *far_ahead
    )

    best = lax.all_to_all(best, "owner", split_axis=0, concat_axis=0, tiled=True)
    best = jnp.broadcast_to(jnp.max(best, axis=0, keepdims=True), (groups, 1, padded))
    arrived = lax.all_to_all(best, "split", split_axis=0, concat_axis=0, tiled=True)

    result = pl.pallas_call(
        functools.partial(pick_kernel, groups),
        out_shape=jax.ShapeDtypeStruct((1, rows), jnp.float32),
        in_specs=[vmem, vmem, vmem],
        out_specs=vmem,
        compiler_params=params,
        name="pick",
    )(arrived, cluster, slots)
    return result.reshape(rows)


def solution(mesh):
    return jax.shard_map(
        shards,
        mesh=mesh,
        in_specs=(
            P(("rep", "owner", "split"), None),
            P(("rep", "owner", "split")),
            P(("rep", "owner", "split")),
        ),
        out_specs=P(("rep", "owner", "split")),
        check_vma=False,
    )
```
